32 devices in a mesh: dp: 4 (over z), expert: 8 (over y, x, core).
Axes of the slice: x: 2, y: 2, z: 4, core: 2. Of those that a mesh axis runs over, the one named last changes fastest.
Arguments:
- tokens: bfloat16 [512, 4096], P(('dp', 'expert')), may hold values from -6 to 6
- units: int32 [512, 8], P(('dp', 'expert')), may hold values from 0 to 23, as said below
- replicas: int32 [8], replicated, may hold values from 0 to 15, as said below
- route_probs: float32 [512, 8], P(('dp', 'expert')), may hold values from 0.05 to 1
- cotangent: bfloat16 [512, 4096], P(('dp', 'expert')), may hold values from -4 to 4
- w_gate: bfloat16 [16, 4096, 768], P('expert', 'dp'), may hold values from -0.09375 to 0.09375
- w_up: bfloat16 [16, 4096, 768], P('expert', 'dp'), may hold values from -0.09375 to 0.09375
- w_down: bfloat16 [16, 768, 4096], P('expert', None, 'dp'), may hold values from -0.21875 to 0.21875
Outputs:
- layer_out: bfloat16 [512, 4096], P(('dp', 'expert'))
- d_tokens: bfloat16 [512, 4096], P(('dp', 'expert'))
- d_probs: float32 [512, 8], P(('dp', 'expert'))
- d_gate_w: bfloat16 [16, 4096, 768], P('expert', 'dp')
- d_up_w: bfloat16 [16, 4096, 768], P('expert', 'dp')
- d_down_w: bfloat16 [16, 768, 4096], P('expert', None, 'dp')
The draws below stay inside these ranges and needn't reach their ends.
Inputs may be any that keep to these rules, and one draw needn't show every extreme that they name: `replicas`: the copy on index o of expert serves one of the 2 experts homed on index (o + 8 - 8 // 2) % 8. `units`: each token's 8 rows name 8 different copies of 8 different experts. Within the rows of one device (aligned blocks of 16 tokens) no copy is named more than 6 times, and in every block some copy is named exactly 6 times.
All inputs are finite; a program needn't handle non-finite values.
Results may differ from the reference program's by a relative error of at most 0.029.
Values may be sent and summed in bfloat16 or wider, within the bound.
A program may use at most 128 MiB of HBM per device.

```python
import math
import jax
import jax.numpy as jnp
from jax import lax

D = 4096
FF = 768
TOP = 8
EXP_DEV = 2
TOK_DEV = 16
EXPERTS = 16
UNITS = 24
CAP = 6
TOKENS = 512
N_DP = 4
N_EXPERT = 8


def shared_plan(key):
    plan_key = jax.random.fold_in(key, 101)
    picks = jax.random.randint(plan_key, (N_EXPERT,), 0, EXP_DEV, dtype=jnp.int32)
    owners_all = jnp.arange(N_EXPERT, dtype=jnp.int32)
    homes = (owners_all + N_EXPERT - N_EXPERT // 2) % N_EXPERT
    return (homes * EXP_DEV + picks).astype(jnp.int32)


def draw_replicas(key, part):
    plan = shared_plan(key)
    return plan.astype(jnp.int32)


def draw_units(key, part):
    plan = shared_plan(key)
    key = jax.random.fold_in(key, 7)
    per_unit = EXP_DEV + 1
    owners_all = jnp.arange(N_EXPERT, dtype=jnp.int32)
    hot_home = (plan // EXP_DEV * per_unit + plan % EXP_DEV).astype(jnp.int32)
    hot_copy = (owners_all * per_unit + EXP_DEV).astype(jnp.int32)
    experts_all = jnp.arange(EXPERTS, dtype=jnp.int32)
    is_hot = jnp.any(experts_all[:, None] == plan[None, :], axis=1).astype(jnp.int32)
    cold_experts = jnp.argsort(is_hot, stable=True)[:EXPERTS - N_EXPERT].astype(jnp.int32)
    cold_units = (cold_experts // EXP_DEV * per_unit + cold_experts % EXP_DEV).astype(jnp.int32)
    half = UNITS // 2
    blocks = TOKENS // TOK_DEV

    def one_block(block_key):
        keys = jax.random.split(block_key, 4)
        order = jax.random.permutation(keys[0], N_EXPERT)
        flips = jax.random.randint(keys[1], (N_EXPERT,), 0, 2, dtype=jnp.int32)
        cold_order = jax.random.permutation(keys[2], EXPERTS - N_EXPERT)
        offset = jax.random.randint(keys[3], (), 0, UNITS, dtype=jnp.int32)
        home_seq = hot_home[order]
        copy_seq = hot_copy[order]
        first = jnp.where(flips == 1, copy_seq, home_seq)
        second = jnp.where(flips == 1, home_seq, copy_seq)
        cold_seq = cold_units[cold_order]
        cycle = jnp.concatenate([first, cold_seq[:half - N_EXPERT], second, cold_seq[half - N_EXPERT:]])
        positions = (offset + jnp.arange(TOK_DEV * TOP, dtype=jnp.int32)) % UNITS
        return cycle[positions]
    block_keys = jax.random.split(key, blocks)
    return jax.vmap(one_block)(block_keys).reshape(TOKENS, TOP).astype(jnp.int32)


def block_scale(key, shape, cuts, low, largest):
    def one(dim, shards_of):
        draws = jax.random.uniform(jax.random.fold_in(jax.random.fold_in(key, 6), dim), (shards_of,), jnp.float32, low / len(cuts), largest / len(cuts))
        return jnp.repeat(jnp.exp(draws), shape[dim] // shards_of).reshape((-1,) + (1,) * (len(shape) - dim - 1))

    gain = one(*cuts[0])
    for cut in cuts[1:]:
        gain = gain * one(*cut)
    return gain


def bell_draw(key, shape, spread, most, cuts=(), kind=jnp.bfloat16):
    array = spread * jax.random.normal(key, shape, jnp.float32)
    if cuts:
        array = array * block_scale(key, shape, cuts, -0.22, 0.18)
    return jnp.clip(array, -most, most).astype(kind)


def setup_inputs(seed: int = 0) -> dict:
    key_of = jax.random.split(jax.random.key(seed), 9)
    tokens = bell_draw(key_of[0], (TOKENS, D), 1.0, 6.0, ((0, 32),))
    units = draw_units(jax.random.fold_in(key_of[8], 71), 0)
    replicas = draw_replicas(jax.random.fold_in(key_of[8], 71), 0)
    route_probs = jnp.clip(jnp.exp(math.log(1.0) - 2.9957323 * jax.random.uniform(key_of[3], (TOKENS, TOP), jnp.float32) ** block_scale(key_of[3], (TOKENS, TOP), ((0, 32),), -0.2, 0.2)), 0.05, 1.0)
    cotangent = bell_draw(key_of[4], (TOKENS, D), 0.25, 4.0, ((0, 32),))
    w_gate = bell_draw(key_of[5], (EXPERTS, D, FF), D ** -0.5, 0.09375, ((0, 8), (1, 4)))
    w_up = bell_draw(key_of[6], (EXPERTS, D, FF), D ** -0.5, 0.09375, ((0, 8), (1, 4)))
    w_down = bell_draw(key_of[7], (EXPERTS, FF, D), FF ** -0.5, 0.21875, ((0, 8), (2, 4)))
    return {"tokens": tokens, "units": units, "replicas": replicas, "route_probs": route_probs, "cotangent": cotangent, "w_gate": w_gate, "w_up": w_up, "w_down": w_down}


def split_sum(row_block, weight_block):
    slot_total = row_block.shape[0]
    row_parts = row_block.astype(jnp.float32).reshape(slot_total, N_DP, D // N_DP)
    weight_parts = weight_block.astype(jnp.float32).reshape(N_DP, D // N_DP, FF)
    partials = jnp.einsum('snd,ndf->snf', row_parts, weight_parts)
    rounded = lax.optimization_barrier(partials.astype(jnp.bfloat16))
    return jnp.sum(rounded.astype(jnp.float32), axis=1)


def split_back(row_block, weight_block):
    slot_total = row_block.shape[0]
    row_parts = row_block.astype(jnp.float32).reshape(slot_total, N_DP, D // N_DP)
    weight_parts = weight_block.astype(jnp.float32).reshape(FF, N_DP, D // N_DP)
    partials = jnp.einsum('snd,fnd->snf', row_parts, weight_parts)
    rounded = lax.optimization_barrier(partials.astype(jnp.bfloat16))
    return jnp.sum(rounded.astype(jnp.float32), axis=1)


def reference(tokens, units, replicas, route_probs, cotangent, w_gate, w_up, w_down):
    per_unit = EXP_DEV + 1
    devices_all = N_DP * N_EXPERT
    row_count = TOK_DEV * TOP
    by_device = units.reshape(devices_all, row_count)
    onehot = (by_device[:, :, None] == jnp.arange(UNITS, dtype=jnp.int32)[None, None, :]).astype(jnp.int32)
    rank_rows = jnp.sum(onehot * (jnp.cumsum(onehot, axis=1) - 1), axis=2)
    slot_ids = (jnp.arange(devices_all, dtype=jnp.int32)[:, None] * CAP + rank_rows).reshape(-1).astype(jnp.int32)
    row_ids = jnp.arange(TOKENS * TOP, dtype=jnp.int32)
    table = jnp.full((UNITS + 1, devices_all * CAP), -1, jnp.int32).at[units.reshape(-1), slot_ids].set(row_ids)
    expert_ids = jnp.arange(EXPERTS, dtype=jnp.int32)
    home_unit = ((expert_ids // EXP_DEV) * per_unit + expert_ids % EXP_DEV).astype(jnp.int32)
    owner_ids = jnp.arange(N_EXPERT, dtype=jnp.int32)
    copy_unit = jnp.full((EXPERTS,), UNITS, jnp.int32).at[replicas].set((owner_ids * per_unit + EXP_DEV).astype(jnp.int32))
    home_table = table[home_unit]
    copy_table = table[copy_unit]
    flat_probs = route_probs.reshape(-1)
    dense_cotangent = cotangent.astype(jnp.float32)

    def unit_pass(totals, slot_rows, weight_gate, weight_up, weight_down):
        out_total, grad_total, prob_total = totals
        filled = slot_rows >= 0
        row_index = jnp.where(filled, slot_rows, 0).astype(jnp.int32)
        token_index = (row_index // TOP).astype(jnp.int32)
        filled_col = filled.astype(jnp.float32)[:, None]
        row_tokens = (tokens[token_index].astype(jnp.float32) * filled_col).astype(jnp.bfloat16)
        row_probs = flat_probs[row_index]
        row_cot = dense_cotangent[token_index]
        scaled_cot = (row_probs[:, None] * row_cot * filled_col).astype(jnp.bfloat16)
        gate_sum = split_sum(row_tokens, weight_gate)
        up_sum = split_sum(row_tokens, weight_up)
        sigmoid_gate = jax.nn.sigmoid(gate_sum)
        silu_gate = gate_sum * sigmoid_gate
        hidden = (silu_gate * up_sum).astype(jnp.bfloat16)
        expert_out = jnp.dot(hidden, weight_down, preferred_element_type=jnp.float32).astype(jnp.bfloat16)
        grad_hidden = split_back(scaled_cot, weight_down)
        grad_gate = (grad_hidden * up_sum * sigmoid_gate * (1.0 + gate_sum * (1.0 - sigmoid_gate))).astype(jnp.bfloat16)
        grad_up = (grad_hidden * silu_gate).astype(jnp.bfloat16)
        down_grad = jnp.dot(hidden.T, scaled_cot, preferred_element_type=jnp.float32)
        gate_grad = jnp.dot(row_tokens.T, grad_gate, preferred_element_type=jnp.float32)
        up_grad = jnp.dot(row_tokens.T, grad_up, preferred_element_type=jnp.float32)
        expert_grad = (jnp.dot(grad_gate, weight_gate.T, preferred_element_type=jnp.float32)
                       + jnp.dot(grad_up, weight_up.T, preferred_element_type=jnp.float32)).astype(jnp.bfloat16)
        out_dense = expert_out.astype(jnp.float32)
        out_total = out_total.at[token_index].add(row_probs[:, None] * out_dense * filled_col)
        grad_total = grad_total.at[token_index].add(expert_grad.astype(jnp.float32) * filled_col)
        prob_total = prob_total.at[row_index].add(jnp.sum(out_dense * row_cot, axis=1) * filled.astype(jnp.float32))
        return (out_total, grad_total, prob_total), (gate_grad, up_grad, down_grad)

    def merge_parts(home_part, copy_part):
        rounded = lax.optimization_barrier(copy_part.astype(jnp.bfloat16))
        return (home_part + rounded.astype(jnp.float32)).astype(jnp.bfloat16)

    def expert_step(totals, pieces):
        home_rows, copy_rows, weight_gate, weight_up, weight_down = pieces
        totals, home_grads = unit_pass(totals, home_rows, weight_gate, weight_up, weight_down)
        totals, copy_grads = unit_pass(totals, copy_rows, weight_gate, weight_up, weight_down)
        merged = (merge_parts(home_grads[0], copy_grads[0]), merge_parts(home_grads[1], copy_grads[1]),
                  merge_parts(home_grads[2], copy_grads[2]))
        return totals, merged

    start = (jnp.zeros((TOKENS, D), jnp.float32), jnp.zeros((TOKENS, D), jnp.float32),
             jnp.zeros((TOKENS * TOP,), jnp.float32))
    finals, grads = lax.scan(expert_step, start, (home_table, copy_table, w_gate, w_up, w_down))
    out_total, grad_total, prob_total = finals
    d_gate_w, d_up_w, d_down_w = grads
    return (out_total.astype(jnp.bfloat16), grad_total.astype(jnp.bfloat16), prob_total.reshape(TOKENS, TOP),
            d_gate_w, d_up_w, d_down_w)
```

```python
import jax
import jax.numpy as jnp
from jax import lax
from jax.sharding import PartitionSpec as P

BF = jnp.bfloat16
F32 = jnp.float32


def dot(spec, a, b):
    return jnp.einsum(spec, a, b, preferred_element_type=F32)


def local(tokens, units, replicas, route_probs, cotangent, w_gate, w_up, w_down):
    groups = lax.axis_size("dp")
    owners = lax.axis_size("expert")
    per_owner = w_gate.shape[0]
    per_unit = per_owner + 1
    unit_total = per_unit * owners
    tok = units.shape[0]
    top = units.shape[1]
    blocks = groups * owners
    total = blocks * tok
    cap = (tok * top + unit_total - 1) // unit_total
    slots = blocks * cap
    width = w_gate.shape[1]
    half = owners // 2
    me = lax.axis_index("expert")
    my_group = lax.axis_index("dp")
    host = (me + half) % owners
    lent = replicas[host] - me * per_owner

    routing = jnp.concatenate([units.astype(F32), route_probs], axis=1)
    routing = lax.all_gather(routing, ("dp", "expert"), axis=0, tiled=True)
    routing = routing.reshape(groups, owners, tok, 2 * top).transpose(1, 0, 2, 3)
    routing = routing.reshape(total, 2 * top)
    all_units = routing[:, :top].astype(jnp.int32)
    all_probs = routing[:, top:]
    both = jnp.concatenate([tokens, cotangent], axis=0)
    both = lax.all_to_all(both, "dp", split_axis=1, concat_axis=0, tiled=True)
    both = lax.all_gather(both, "expert", axis=0, tiled=True)
    both = both.reshape(blocks, 2, tok, width)
    all_tokens = both[:, 0].reshape(total, width)
    all_cot = both[:, 1].reshape(total, width)

    mine = jnp.concatenate(
        [
            me * per_unit + jnp.arange(per_owner, dtype=jnp.int32),
            (host * per_unit + per_owner)[None].astype(jnp.int32),
        ]
    )
    match = all_units[None] == mine[:, None, None]
    named = jnp.any(match, axis=2)
    unit_probs = jnp.sum(jnp.where(match, all_probs[None], 0.0), axis=2)
    by_block = named.reshape(per_unit, blocks, tok).astype(jnp.int32)
    earlier = (
        jnp.arange(tok, dtype=jnp.int32)[:, None] < jnp.arange(tok, dtype=jnp.int32)[None, :]
    ).astype(jnp.int32)
    rank = jnp.sum(by_block[:, :, :, None] * earlier, axis=2)
    slot = (rank + jnp.arange(blocks, dtype=jnp.int32)[None, :, None] * cap).reshape(
        per_unit, total
    )
    slot = jnp.where(named, slot, -1)
    chosen = slot[:, None, :] == jnp.arange(slots, dtype=jnp.int32)[None, :, None]
    select = chosen.astype(BF)
    slot_probs = jnp.sum(jnp.where(chosen, unit_probs[:, None, :], 0.0), axis=2)

    flat_select = select.reshape(per_unit * slots, total)
    xs = dot("st,td->sd", flat_select, all_tokens).astype(BF).reshape(per_unit, slots, width)
    ds = (
        slot_probs.reshape(-1)[:, None] * dot("st,td->sd", flat_select, all_cot)
    ).astype(BF).reshape(per_unit, slots, width)

    def at(weights, u):
        if u < per_owner:
            return weights[u]
        return lax.dynamic_index_in_dim(weights, lent, 0, keepdims=False)

    def per(spec, rows, weights):
        return jnp.stack(
            [dot(spec, rows[u], at(weights, u)).astype(BF) for u in range(per_unit)]
        )

    gate, up, grad_hidden = lax.psum(
        (
            per("sd,df->sf", xs, w_gate),
            per("sd,df->sf", xs, w_up),
            per("sd,fd->sf", ds, w_down),
        ),
        "dp",
    )
    gate, up, grad_hidden = gate.astype(F32), up.astype(F32), grad_hidden.astype(F32)
    sig = jax.nn.sigmoid(gate)
    silu = gate * sig
    hidden = (silu * up).astype(BF)
    grad_gate = (grad_hidden * up * sig * (1.0 + gate * (1.0 - sig))).astype(BF)
    grad_up = (grad_hidden * silu).astype(BF)

    def send_back(rows):
        part = dot("st,sd->td", flat_select, rows.reshape(per_unit * slots, width)).astype(BF)
        part = lax.all_to_all(part, "expert", split_axis=0, concat_axis=0, tiled=True)
        part = part.reshape(owners, groups, tok, width)
        return jnp.sum(part.astype(F32), axis=0).astype(BF)

    expert_out = jnp.stack([dot("sf,fd->sd", hidden[u], at(w_down, u)) for u in range(per_unit)])
    out_part = send_back((slot_probs[:, :, None] * expert_out).astype(BF))
    expert_grad = jnp.stack(
        [
            (
                dot("sf,df->sd", grad_gate[u], at(w_gate, u))
                + dot("sf,df->sd", grad_up[u], at(w_up, u))
            ).astype(BF)
            for u in range(per_unit)
        ]
    )
    grad_part = send_back(expert_grad)
    last = jnp.concatenate([out_part, grad_part], axis=1).reshape(groups * 2 * tok, width)
    last = lax.all_to_all(last, "dp", split_axis=0, concat_axis=1, tiled=True)
    layer_out = last[:tok]
    d_tokens = last[tok:]

    filled = slot_probs > 0.0
    dots = jnp.sum(hidden.astype(F32) * grad_hidden, axis=2) / jnp.where(filled, slot_probs, 1.0)
    per_token = jnp.sum(jnp.where(chosen, dots[:, :, None], 0.0), axis=1)
    spread = jnp.sum(jnp.where(match, per_token[:, :, None], 0.0), axis=0)
    spread = lax.dynamic_index_in_dim(
        spread.reshape(owners, groups, tok, top), my_group, 1, keepdims=False
    )
    spread = lax.all_to_all(spread, "expert", split_axis=0, concat_axis=0, tiled=True)
    d_probs = jnp.sum(spread, axis=0)

    def weight_grads(left, right):
        grads = []
        for e in range(per_owner):
            marked = jnp.where(lent == e, 1.0, 0.0).astype(BF)
            a = jnp.concatenate([left[e], left[per_owner]], axis=0)
            b = jnp.concatenate([right[e], right[per_owner] * marked], axis=0)
            grads.append(dot("sa,sb->ab", a, b).astype(BF))
        return jnp.stack(grads)

    d_gate_w = weight_grads(xs, grad_gate)
    d_up_w = weight_grads(xs, grad_up)
    d_down_w = weight_grads(hidden, ds)
    return (layer_out, d_tokens, d_probs, d_gate_w, d_up_w, d_down_w)


def solution(mesh):
    rows = P(("dp", "expert"), None)
    weights = P("expert", "dp", None)
    down = P("expert", None, "dp")
    return jax.shard_map(
        local,
        mesh=mesh,
        in_specs=(rows, rows, P(), rows, rows, weights, weights, down),
        out_specs=(rows, rows, rows, weights, weights, down),
        check_vma=False,
    )
```

```python
import jax
import jax.numpy as jnp
from jax import lax
from jax.sharding import PartitionSpec as P

BF = jnp.bfloat16
F32 = jnp.float32


def dot(spec, a, b):
    return jnp.einsum(spec, a, b, preferred_element_type=F32)


def local(tokens, units, replicas, route_probs, cotangent, w_gate, w_up, w_down):
    groups = lax.axis_size("dp")
    owners = lax.axis_size("expert")
    per_owner = w_gate.shape[0]
    per_unit = per_owner + 1
    unit_total = per_unit * owners
    tok = units.shape[0]
    top = units.shape[1]
    blocks = groups * owners
    total = blocks * tok
    cap = (tok * top + unit_total - 1) // unit_total
    slots = blocks * cap
    width = w_gate.shape[1]
    half = owners // 2
    me = lax.axis_index("expert")
    my_group = lax.axis_index("dp")
    host = (me + half) % owners
    lent = replicas[host] - me * per_owner

    routing = jnp.concatenate([units.astype(F32), route_probs], axis=1)
    routing = lax.all_gather(routing, ("dp", "expert"), axis=0, tiled=True)
    routing = routing.reshape(groups, owners, tok, 2 * top).transpose(1, 0, 2, 3)
    routing = routing.reshape(total, 2 * top)
    all_units = routing[:, :top].astype(jnp.int32)
    all_probs = routing[:, top:]
    both = jnp.concatenate([tokens, cotangent], axis=0)
    both = lax.all_to_all(both, "dp", split_axis=1, concat_axis=0, tiled=True)
    both = both.reshape(groups, 2, tok, width)

    def gathered(rows):
        return lax.all_gather(rows.reshape(groups * tok, width), "expert", axis=0, tiled=True)

    all_tokens = gathered(both[:, 0])
    cot_rows, all_tokens = lax.optimization_barrier((both[:, 1], all_tokens))
    all_cot = gathered(cot_rows)

    mine = jnp.concatenate(
        [
            me * per_unit + jnp.arange(per_owner, dtype=jnp.int32),
            (host * per_unit + per_owner)[None].astype(jnp.int32),
        ]
    )
    match = all_units[None] == mine[:, None, None]
    named = jnp.any(match, axis=2)
    unit_probs = jnp.sum(jnp.where(match, all_probs[None], 0.0), axis=2)
    by_block = named.reshape(per_unit, blocks, tok).astype(jnp.int32)
    earlier = (
        jnp.arange(tok, dtype=jnp.int32)[:, None] < jnp.arange(tok, dtype=jnp.int32)[None, :]
    ).astype(jnp.int32)
    rank = jnp.sum(by_block[:, :, :, None] * earlier, axis=2)
    slot = (rank + jnp.arange(blocks, dtype=jnp.int32)[None, :, None] * cap).reshape(
        per_unit, total
    )
    slot = jnp.where(named, slot, -1)
    chosen = slot[:, None, :] == jnp.arange(slots, dtype=jnp.int32)[None, :, None]
    select = chosen.astype(BF)
    slot_probs = jnp.sum(jnp.where(chosen, unit_probs[:, None, :], 0.0), axis=2)

    flat_select = select.reshape(per_unit * slots, total)
    xs = dot("st,td->sd", flat_select, all_tokens).astype(BF).reshape(per_unit, slots, width)
    ds = (
        slot_probs.reshape(-1)[:, None] * dot("st,td->sd", flat_select, all_cot)
    ).astype(BF).reshape(per_unit, slots, width)

    def at(weights, u):
        if u < per_owner:
            return weights[u]
        return lax.dynamic_index_in_dim(weights, lent, 0, keepdims=False)

    def per(spec, rows, weights):
        return jnp.stack(
            [dot(spec, rows[u], at(weights, u)).astype(BF) for u in range(per_unit)]
        )

    gate, up = lax.psum((per("sd,df->sf", xs, w_gate), per("sd,df->sf", xs, w_up)), "dp")
    partial_grad, gate, up = lax.optimization_barrier((per("sd,fd->sf", ds, w_down), gate, up))
    grad_hidden = lax.psum(partial_grad, "dp")
    gate, up, grad_hidden = gate.astype(F32), up.astype(F32), grad_hidden.astype(F32)
    sig = jax.nn.sigmoid(gate)
    silu = gate * sig
    hidden = (silu * up).astype(BF)
    grad_gate = (grad_hidden * up * sig * (1.0 + gate * (1.0 - sig))).astype(BF)
    grad_up = (grad_hidden * silu).astype(BF)

    def send_back(rows):
        part = dot("st,sd->td", flat_select, rows.reshape(per_unit * slots, width)).astype(BF)
        part = lax.all_to_all(part, "expert", split_axis=0, concat_axis=0, tiled=True)
        part = part.reshape(owners, groups, tok, width)
        return jnp.sum(part.astype(F32), axis=0).astype(BF)

    expert_out = jnp.stack([dot("sf,fd->sd", hidden[u], at(w_down, u)) for u in range(per_unit)])
    out_part = send_back((slot_probs[:, :, None] * expert_out).astype(BF))
    expert_grad = jnp.stack(
        [
            (
                dot("sf,df->sd", grad_gate[u], at(w_gate, u))
                + dot("sf,df->sd", grad_up[u], at(w_up, u))
            ).astype(BF)
            for u in range(per_unit)
        ]
    )
    grad_part = send_back(expert_grad)
    last = jnp.concatenate([out_part, grad_part], axis=1).reshape(groups * 2 * tok, width)
    last = lax.all_to_all(last, "dp", split_axis=0, concat_axis=1, tiled=True)
    layer_out = last[:tok]
    d_tokens = last[tok:]

    filled = slot_probs > 0.0
    dots = jnp.sum(hidden.astype(F32) * grad_hidden, axis=2) / jnp.where(filled, slot_probs, 1.0)
    per_token = jnp.sum(jnp.where(chosen, dots[:, :, None], 0.0), axis=1)
    spread = jnp.sum(jnp.where(match, per_token[:, :, None], 0.0), axis=0)
    spread = lax.dynamic_index_in_dim(
        spread.reshape(owners, groups, tok, top), my_group, 1, keepdims=False
    )
    spread = lax.all_to_all(spread, "expert", split_axis=0, concat_axis=0, tiled=True)
    d_probs = jnp.sum(spread, axis=0)

    def weight_grads(left, right):
        grads = []
        for e in range(per_owner):
            marked = jnp.where(lent == e, 1.0, 0.0).astype(BF)
            a = jnp.concatenate([left[e], left[per_owner]], axis=0)
            b = jnp.concatenate([right[e], right[per_owner] * marked], axis=0)
            grads.append(dot("sa,sb->ab", a, b).astype(BF))
        return jnp.stack(grads)

    d_gate_w = weight_grads(xs, grad_gate)
    d_up_w = weight_grads(xs, grad_up)
    d_down_w = weight_grads(hidden, ds)
    return (layer_out, d_tokens, d_probs, d_gate_w, d_up_w, d_down_w)


def solution(mesh):
    rows = P(("dp", "expert"), None)
    weights = P("expert", "dp", None)
    down = P("expert", None, "dp")
    return jax.shard_map(
        local,
        mesh=mesh,
        in_specs=(rows, rows, P(), rows, rows, weights, weights, down),
        out_specs=(rows, rows, rows, weights, weights, down),
        check_vma=False,
    )
```

```python
import jax
import jax.numpy as jnp
from jax import lax
from jax.sharding import PartitionSpec as P

BF = jnp.bfloat16
F32 = jnp.float32


def dot(spec, a, b):
    return jnp.einsum(spec, a, b, preferred_element_type=F32)


def local(tokens, units, replicas, route_probs, cotangent, w_gate, w_up, w_down):
    groups = lax.axis_size("dp")
    owners = lax.axis_size("expert")
    per_owner = w_gate.shape[0]
    per_unit = per_owner + 1
    unit_total = per_unit * owners
    tok = units.shape[0]
    top = units.shape[1]
    blocks = groups * owners
    total = blocks * tok
    cap = (tok * top + unit_total - 1) // unit_total
    slots = blocks * cap
    width = w_gate.shape[1]
    half = owners // 2
    me = lax.axis_index("expert")
    my_group = lax.axis_index("dp")
    host = (me + half) % owners
    lent = replicas[host] - me * per_owner

    high = lax.reduce_precision(route_probs, 8, 7)
    middle = lax.reduce_precision(route_probs - high, 8, 7)
    low = route_probs - high - middle
    routing = jnp.concatenate([units.astype(F32), high, middle, low], axis=1).astype(BF)
    side = 128 * ((4 * top + 127) // 128)
    routing = jnp.pad(routing, ((0, 0), (0, side - 4 * top)))
    rows = jnp.concatenate([tokens, cotangent], axis=0)
    routing = jnp.concatenate([routing, jnp.zeros_like(routing)], axis=0)
    pieces = []
    for g in range(groups):
        pieces.append(
            jnp.concatenate([rows[:, g * width : (g + 1) * width], routing], axis=1)
        )
    both = jnp.concatenate(pieces, axis=0)
    both = lax.all_to_all(both, "dp", split_axis=0, concat_axis=0, tiled=True)
    both = lax.all_gather(both, "expert", axis=0, tiled=True)
    both = both.reshape(blocks, 2, tok, width + side)
    all_tokens = both[:, 0, :, :width].reshape(total, width)
    all_cot = both[:, 1, :, :width].reshape(total, width)
    routing = both[:, 0, :, width : width + 4 * top].reshape(total, 4, top).astype(F32)
    all_units = routing[:, 0].astype(jnp.int32)
    all_probs = routing[:, 1] + routing[:, 2] + routing[:, 3]

    mine = jnp.concatenate(
        [
            me * per_unit + jnp.arange(per_owner, dtype=jnp.int32),
            (host * per_unit + per_owner)[None].astype(jnp.int32),
        ]
    )
    match = all_units[None] == mine[:, None, None]
    named = jnp.any(match, axis=2)
    unit_probs = jnp.sum(jnp.where(match, all_probs[None], 0.0), axis=2)
    by_block = named.reshape(per_unit, blocks, tok).astype(jnp.int32)
    earlier = (
        jnp.arange(tok, dtype=jnp.int32)[:, None] < jnp.arange(tok, dtype=jnp.int32)[None, :]
    ).astype(jnp.int32)
    rank = jnp.sum(by_block[:, :, :, None] * earlier, axis=2)
    slot = (rank + jnp.arange(blocks, dtype=jnp.int32)[None, :, None] * cap).reshape(
        per_unit, total
    )
    slot = jnp.where(named, slot, -1)
    chosen = slot[:, None, :] == jnp.arange(slots, dtype=jnp.int32)[None, :, None]
    select = chosen.astype(BF)
    slot_probs = jnp.sum(jnp.where(chosen, unit_probs[:, None, :], 0.0), axis=2)

    flat_select = select.reshape(per_unit * slots, total)
    xs = dot("st,td->sd", flat_select, all_tokens).astype(BF).reshape(per_unit, slots, width)
    ds = (
        slot_probs.reshape(-1)[:, None] * dot("st,td->sd", flat_select, all_cot)
    ).astype(BF).reshape(per_unit, slots, width)

    def at(weights, u):
        if u < per_owner:
            return weights[u]
        return lax.dynamic_index_in_dim(weights, lent, 0, keepdims=False)

    def per(spec, rows, weights):
        return jnp.stack(
            [dot(spec, rows[u], at(weights, u)).astype(BF) for u in range(per_unit)]
        )

    gate, up, grad_hidden = lax.psum(
        (
            per("sd,df->sf", xs, w_gate),
            per("sd,df->sf", xs, w_up),
            per("sd,fd->sf", ds, w_down),
        ),
        "dp",
    )
    gate, up, grad_hidden = gate.astype(F32), up.astype(F32), grad_hidden.astype(F32)
    sig = jax.nn.sigmoid(gate)
    silu = gate * sig
    hidden = (silu * up).astype(BF)
    grad_gate = (grad_hidden * up * sig * (1.0 + gate * (1.0 - sig))).astype(BF)
    grad_up = (grad_hidden * silu).astype(BF)

    filled = slot_probs > 0.0
    dots = jnp.sum(hidden.astype(F32) * grad_hidden, axis=2) / jnp.where(filled, slot_probs, 1.0)
    per_token = jnp.sum(jnp.where(chosen, dots[:, :, None], 0.0), axis=1)
    spread = jnp.sum(jnp.where(match, per_token[:, :, None], 0.0), axis=0)
    spread_high = lax.reduce_precision(spread, 8, 7)
    spread = jnp.concatenate([spread_high, spread - spread_high], axis=1).astype(BF)
    spread = jnp.pad(spread, ((0, 0), (0, side - 2 * top)))

    def combined(rows):
        return dot("st,sd->td", flat_select, rows.reshape(per_unit * slots, width)).astype(BF)

    def send_back(part):
        part = lax.all_to_all(part, "expert", split_axis=0, concat_axis=0, tiled=True)
        part = part.reshape(owners, groups, tok, -1)
        return jnp.sum(part.astype(F32), axis=0)

    expert_out = jnp.stack([dot("sf,fd->sd", hidden[u], at(w_down, u)) for u in range(per_unit)])
    out_part = combined((slot_probs[:, :, None] * expert_out).astype(BF))
    out_part = send_back(jnp.concatenate([out_part, spread], axis=1))
    d_probs = lax.dynamic_index_in_dim(out_part[:, :, width:], my_group, 0, keepdims=False)
    d_probs = d_probs[:, :top] + d_probs[:, top : 2 * top]
    out_part = out_part[:, :, :width].astype(BF)
    expert_grad = jnp.stack(
        [
            (
                dot("sf,df->sd", grad_gate[u], at(w_gate, u))
                + dot("sf,df->sd", grad_up[u], at(w_up, u))
            ).astype(BF)
            for u in range(per_unit)
        ]
    )
    grad_part = send_back(combined(expert_grad)).astype(BF)
    last = jnp.concatenate([out_part, grad_part], axis=1).reshape(groups * 2 * tok, width)
    last = lax.all_to_all(last, "dp", split_axis=0, concat_axis=1, tiled=True)
    layer_out = last[:tok]
    d_tokens = last[tok:]

    def weight_grads(left, right):
        marked = (jnp.arange(per_owner, dtype=jnp.int32) == lent).astype(BF)[:, None, None]
        extra = jnp.broadcast_to(left[per_owner:], left[:per_owner].shape)
        a = jnp.concatenate([left[:per_owner], extra], axis=1)
        b = jnp.concatenate([right[:per_owner], right[per_owner:] * marked], axis=1)
        return dot("esa,esb->eab", a, b).astype(BF)

    d_gate_w = weight_grads(xs, grad_gate)
    d_up_w = weight_grads(xs, grad_up)
    d_down_w = weight_grads(hidden, ds)
    return (layer_out, d_tokens, d_probs, d_gate_w, d_up_w, d_down_w)


def solution(mesh):
    rows = P(("dp", "expert"), None)
    weights = P("expert", "dp", None)
    down = P("expert", None, "dp")
    return jax.shard_map(
        local,
        mesh=mesh,
        in_specs=(rows, rows, P(), rows, rows, weights, weights, down),
        out_specs=(rows, rows, rows, weights, weights, down),
        check_vma=False,
    )
```
